128 devices in a mesh: leaf: 2 (over core), prow: 2 (over x_hi), pcol: 32 (over z, y, x_lo).
Axes of the slice: x: 4 (x_hi: 2, x_lo: 2; x = x_hi * 2 + x_lo), y: 4, z: 4, core: 2. Of those that a mesh axis runs over, the one named last changes fastest.
Arguments:
- known_above: bfloat16 [2, 2, 256, 256], P('prow'), may hold values from -6 to 6
- seed_top: float32 [2, 2, 32, 2, 256, 256], P('leaf', 'prow', 'pcol'), may hold values from -6 to 6
- seed_mid: float32 [2, 2, 32, 2, 256, 256], P('leaf', 'prow', 'pcol'), may hold values from -6 to 6
- seed_low: float32 [2, 2, 32, 2, 256, 256], P('leaf', 'prow', 'pcol'), may hold values from -6 to 6
- inverse_top: bfloat16 [2, 2, 32, 2, 256, 256], P('leaf', 'prow', 'pcol'), may hold values from -0.375 to 0.375
- middle_inverses: bfloat16 [2, 2, 32, 2, 256, 256], P('leaf', 'prow', 'pcol'), may hold values from -0.375 to 0.375
- inverse_low: bfloat16 [2, 2, 32, 2, 256, 256], P('leaf', 'prow', 'pcol'), may hold values from -0.375 to 0.375
- tiles_top: bfloat16 [2, 2, 32, 58, 256, 256], P('leaf', 'prow', 'pcol'), may hold values from -0.046875 to 0.046875
- tiles_mid: bfloat16 [2, 2, 32, 58, 256, 256], P('leaf', 'prow', 'pcol'), may hold values from -0.046875 to 0.046875
- tiles_low: bfloat16 [2, 2, 32, 58, 256, 256], P('leaf', 'prow', 'pcol'), may hold values from -0.046875 to 0.046875
- top_source_rows: int32 [2, 2, 32, 58], P('leaf', 'prow', 'pcol'), may hold values from 0 to 1
- source_mid: int32 [2, 2, 32, 58], P('leaf', 'prow', 'pcol'), may hold values from 0 to 129
- lowest_source_rows: int32 [2, 2, 32, 58], P('leaf', 'prow', 'pcol'), may hold values from 0 to 193
- target_top: int32 [2, 2, 32, 58], P('leaf', 'prow', 'pcol'), may hold values from 0 to 3
- target_mid: int32 [2, 2, 32, 58], P('leaf', 'prow', 'pcol'), may hold values from 0 to 3
- target_low: int32 [2, 2, 32, 58], P('leaf', 'prow', 'pcol'), may hold values from 0 to 3
Outputs:
- solved_top: float32 [2, 2, 32, 2, 256, 256], P('leaf', 'prow', 'pcol')
- solved_mid: float32 [2, 2, 32, 2, 256, 256], P('leaf', 'prow', 'pcol')
- solved_low: float32 [2, 2, 32, 2, 256, 256], P('leaf', 'prow', 'pcol')
The draws below stay inside these ranges and needn't reach their ends.
All inputs are finite; a program needn't handle non-finite values.
Results may differ from the reference program's by a relative error of at most 0.015.
Values may be sent and summed in bfloat16 or wider, within the bound.
No kernel may reach another device: no remote copies, remote signals or barrier semaphores. Data moves between devices by JAX's collectives and lax.ppermute only.
A program may use at most 192 MiB of HBM per device.

```python
import jax
import jax.numpy as jnp
from jax import lax

NS = 256
R = 256
TILES = 58
CBD = 2
UPD = 2
CB = 4
ROWS_MID = 130
ROWS_LOW = 194
N_LEAF = 2
N_PROW = 2
N_PCOL = 32


def place_ends(result, own_key, smallest, high):
    longest = result.shape.index(max(result.shape))
    spots = []
    for shift in (0, 1):
        where = [jax.random.randint(jax.random.fold_in(own_key, axis), (), 0, length) for axis, length in enumerate(result.shape)]
        where[longest] = (where[longest] + shift) % result.shape[longest]
        spots.append(tuple(where))
    return result.at[spots[0]].set(smallest).at[spots[1]].set(high)


def shard_levels(own_key, extent, pieces, low, largest):
    gain = 1.0
    for position, blocks in pieces:
        heights = jax.random.uniform(jax.random.fold_in(jax.random.fold_in(own_key, 6), position), (blocks,), jnp.float32, low / len(pieces), largest / len(pieces))
        gain = gain * jnp.repeat(jnp.exp(heights), extent[position] // blocks).reshape((-1,) + (1,) * (len(extent) - 1 - position))
    return gain


def centred(key, dims, deviation, most, split=(), kind=jnp.bfloat16):
    drawn = deviation * jax.random.normal(key, dims, jnp.float32)
    if split:
        drawn = drawn * shard_levels(key, dims, split, -0.22, 0.18)
    return jnp.clip(drawn, -most, most).astype(kind)


def setup_inputs(seed: int = 0) -> dict:
    arg_keys = jax.random.split(jax.random.key(seed), 17)
    return {
        "known_above": centred(arg_keys[0], (N_PROW, UPD, R, NS), 1.0, 6.0, ((0, 2),)),
        "seed_top": centred(arg_keys[1], (N_LEAF, N_PROW, N_PCOL, CBD, R, NS), 1.0, 6.0, ((0, 2), (1, 2), (2, 32)), jnp.float32),
        "seed_mid": centred(arg_keys[2], (N_LEAF, N_PROW, N_PCOL, CBD, R, NS), 1.0, 6.0, ((0, 2), (1, 2), (2, 32)), jnp.float32),
        "seed_low": centred(arg_keys[3], (N_LEAF, N_PROW, N_PCOL, CBD, R, NS), 1.0, 6.0, ((0, 2), (1, 2), (2, 32)), jnp.float32),
        "inverse_top": centred(arg_keys[4], (N_LEAF, N_PROW, N_PCOL, CBD, NS, NS), NS ** -0.5, 0.375, ((0, 2), (1, 2), (2, 32))),
        "middle_inverses": centred(arg_keys[5], (N_LEAF, N_PROW, N_PCOL, CBD, NS, NS), NS ** -0.5, 0.375, ((0, 2), (1, 2), (2, 32))),
        "inverse_low": centred(arg_keys[6], (N_LEAF, N_PROW, N_PCOL, CBD, NS, NS), NS ** -0.5, 0.375, ((0, 2), (1, 2), (2, 32))),
        "tiles_top": centred(arg_keys[7], (N_LEAF, N_PROW, N_PCOL, TILES, NS, NS), (2 * TILES * NS // CBD) ** -0.5, 0.046875, ((0, 2), (1, 2), (2, 32))),
        "tiles_mid": centred(arg_keys[8], (N_LEAF, N_PROW, N_PCOL, TILES, NS, NS), (2 * TILES * NS // CBD) ** -0.5, 0.046875, ((0, 2), (1, 2), (2, 32))),
        "tiles_low": centred(arg_keys[9], (N_LEAF, N_PROW, N_PCOL, TILES, NS, NS), (2 * TILES * NS // CBD) ** -0.5, 0.046875, ((0, 2), (1, 2), (2, 32))),
        "top_source_rows": place_ends(jax.random.randint(arg_keys[10], (N_LEAF, N_PROW, N_PCOL, TILES), 0, UPD), jax.random.fold_in(arg_keys[10], 1), 0, UPD - 1).astype(jnp.int32),
        "source_mid": place_ends(jax.random.randint(arg_keys[11], (N_LEAF, N_PROW, N_PCOL, TILES), 0, ROWS_MID), jax.random.fold_in(arg_keys[11], 1), 0, ROWS_MID - 1).astype(jnp.int32),
        "lowest_source_rows": place_ends(jax.random.randint(arg_keys[12], (N_LEAF, N_PROW, N_PCOL, TILES), 0, ROWS_LOW), jax.random.fold_in(arg_keys[12], 1), 0, ROWS_LOW - 1).astype(jnp.int32),
        "target_top": place_ends(jax.random.randint(arg_keys[13], (N_LEAF, N_PROW, N_PCOL, TILES), 0, CB), jax.random.fold_in(arg_keys[13], 1), 0, CB - 1).astype(jnp.int32),
        "target_mid": place_ends(jax.random.randint(arg_keys[14], (N_LEAF, N_PROW, N_PCOL, TILES), 0, CB), jax.random.fold_in(arg_keys[14], 1), 0, CB - 1).astype(jnp.int32),
        "target_low": place_ends(jax.random.randint(arg_keys[15], (N_LEAF, N_PROW, N_PCOL, TILES), 0, CB), jax.random.fold_in(arg_keys[15], 1), 0, CB - 1).astype(jnp.int32),
    }


def level_solve(row_list, tiles, source, target, right_side, inverse):
    n_leaf, n_prow, n_pcol, count_tiles = source.shape
    per_dev = right_side.shape[3]
    columns = n_prow * per_dev
    width = right_side.shape[4]
    depth = right_side.shape[5]
    leaf_ids = jnp.arange(n_leaf, dtype=jnp.int32)[:, None, None]

    def one_prow(acc, items):
        tile_block, src, tgt, rows_here = items
        picked = rows_here[leaf_ids, src]
        products = jnp.einsum("lctra,lctab->lctrb", picked.astype(jnp.float32), tile_block.astype(jnp.float32), precision=lax.Precision.HIGHEST)
        choice_mask = (tgt[:, :, None, :] == jnp.arange(columns, dtype=jnp.int32)[None, None, :, None]).astype(jnp.float32)
        part = jnp.einsum("lcmt,lctrb->lcmrb", choice_mask, products, precision=lax.Precision.HIGHEST)
        part = lax.optimization_barrier(part.astype(jnp.bfloat16)).astype(jnp.float32)
        return acc + part, None

    start = jnp.zeros((n_leaf, n_pcol, columns, width, depth), jnp.float32)
    items = (jnp.transpose(tiles, (1, 0, 2, 3, 4, 5)), jnp.transpose(source, (1, 0, 2, 3)), jnp.transpose(target, (1, 0, 2, 3)), row_list)
    total, unused = lax.scan(one_prow, start, items)
    sums = jnp.transpose(total.reshape(n_leaf, n_pcol, n_prow, per_dev, width, depth), (0, 2, 1, 3, 4, 5))
    reduced = (right_side - sums).astype(jnp.bfloat16)
    return jnp.einsum("lpcdrb,lpcdab->lpcdra", reduced.astype(jnp.float32), inverse.astype(jnp.float32), precision=lax.Precision.HIGHEST)


def extend_shared(row_list, solved_state):
    n_leaf, n_prow, n_pcol, per_dev, width, depth = solved_state.shape
    rounded = solved_state.astype(jnp.bfloat16)
    fresh = jnp.transpose(rounded, (1, 0, 2, 3, 4, 5)).reshape(n_prow, 1, n_leaf * n_pcol * per_dev, width, depth)
    fresh = jnp.broadcast_to(fresh, (n_prow, n_leaf, n_leaf * n_pcol * per_dev, width, depth))
    return jnp.concatenate([row_list, fresh], axis=2)


def extend_own(row_list, solved_state):
    n_leaf, n_prow, n_pcol, per_dev, width, depth = solved_state.shape
    rounded = solved_state.astype(jnp.bfloat16)
    fresh = jnp.transpose(rounded, (1, 0, 2, 3, 4, 5)).reshape(n_prow, n_leaf, n_pcol * per_dev, width, depth)
    return jnp.concatenate([row_list, fresh], axis=2)


def reference(known_above, seed_top, seed_mid, seed_low, inverse_top, middle_inverses, inverse_low, tiles_top, tiles_mid, tiles_low, top_source_rows, source_mid, lowest_source_rows, target_top, target_mid, target_low):
    n_leaf = seed_top.shape[0]
    n_prow, upper, width, depth = known_above.shape
    row_list = jnp.broadcast_to(known_above[:, None], (n_prow, n_leaf, upper, width, depth))
    solved_top = level_solve(row_list, tiles_top, top_source_rows, target_top, seed_top, inverse_top)
    row_list = extend_shared(row_list, solved_top)
    solved_mid = level_solve(row_list, tiles_mid, source_mid, target_mid, seed_mid, middle_inverses)
    row_list = extend_own(row_list, solved_mid)
    solved_low = level_solve(row_list, tiles_low, lowest_source_rows, target_low, seed_low, inverse_low)
    return (solved_top, solved_mid, solved_low)
```

```python
import functools

import jax
import jax.numpy as jnp
from jax import lax
from jax.experimental import pallas as pl
from jax.experimental.pallas import tpu as pltpu
from jax.sharding import PartitionSpec as P

BF16 = jnp.bfloat16
F32 = jnp.float32


def products_kernel(columns, stores_of, with_init, *refs):
    order, loc, starts = refs[:3]
    n_stores = 1 + max(store for _, store in stores_of)
    stores = refs[3 : 3 + n_stores]
    refs = refs[3 + n_stores :]
    tiles, refs = refs[0], refs[1:]
    if with_init:
        init, refs = refs[0], refs[1:]
    out, row_buf, tile_buf, acc, sem = refs
    depth = tiles.shape[1]

    def at(i, n=1):
        return pl.ds(pl.multiple_of(i * depth, depth), n * depth)

    def row_copy(store, i):
        return pltpu.make_async_copy(stores[store].at[loc[i]], row_buf.at[:, at(i)], sem.at[i])

    def tile_copy(i):
        return pltpu.make_async_copy(tiles.at[order[i]], tile_buf.at[at(i)], sem.at[i])

    for base in columns:
        for group, store in stores_of:

            def issue(i, carry, store=store):
                tile_copy(i).start()
                row_copy(store, i).start()
                return carry

            lax.fori_loop(starts[base + group], starts[base + group + 1], issue, 0)

    if with_init:
        acc[...] = init[...]
    else:
        acc[...] = jnp.zeros_like(acc)

    for c, base in enumerate(columns):
        first = starts[base + stores_of[0][0]]
        last = starts[base + stores_of[-1][0] + 1]

        def multiply(i, n, c=c):
            for k in range(n):
                both = tile_buf.at[pl.ds(0, depth + row_buf.shape[0])]
                pltpu.make_async_copy(both, both, sem.at[i + k]).wait()
            acc[c] += jnp.dot(row_buf[:, at(i, n)], tile_buf[at(i, n)], preferred_element_type=F32)

        def several(j, carry, first=first, multiply=multiply):
            multiply(first + RUN * j, RUN)
            return carry

        runs = (last - first) // RUN
        lax.fori_loop(0, runs, several, 0)
        first = first + runs * RUN
        size = RUN // 2
        while size:

            def rest(j, carry, first=first, size=size, multiply=multiply):
                multiply(first, size)
                return carry

            some = (last - first) // size
            lax.fori_loop(0, some, rest, 0)
            first = first + some * size
            size //= 2
    out[...] = acc[...].astype(out.dtype)


RUN = 4


def tile_products(index, columns, stores_of, stores, tiles, out_dtype, init=None):
    order, loc, starts = index
    count, depth, width = tiles.shape
    rows = stores[0].shape[1]
    in_hbm = pl.BlockSpec(memory_space=pltpu.HBM)
    in_vmem = pl.BlockSpec(memory_space=pltpu.VMEM)
    in_smem = pl.BlockSpec(memory_space=pltpu.SMEM)
    operands = [order, loc, starts, *stores, tiles]
    specs = [in_smem] * 3 + [in_hbm] * (len(stores) + 1)
    if init is not None:
        operands.append(init)
        specs.append(in_vmem)
    return pl.pallas_call(
        functools.partial(products_kernel, tuple(columns), tuple(stores_of), init is not None),
        out_shape=jax.ShapeDtypeStruct((len(columns), rows, width), out_dtype),
        in_specs=specs,
        out_specs=in_vmem,
        scratch_shapes=[
            pltpu.VMEM((rows, count * depth), BF16),
            pltpu.VMEM((count * depth, width), BF16),
            pltpu.VMEM((len(columns), rows, width), F32),
            pltpu.SemaphoreType.DMA((count,)),
        ],
        compiler_params=pltpu.CompilerParams(vmem_limit_bytes=60 * 1024 * 1024),
        cost_estimate=pl.CostEstimate(
            flops=count * rows * depth * width, bytes_accessed=count * depth * width * 2, transcendentals=0
        ),
    )(*operands)


def top_kernel(per_dev, row, source, target, known, tiles, away, mine, tile_buf, total, tile_sem):
    count = tiles.shape[0]
    upper, depth = known.shape[0], known.shape[2]

    def tile_copy(i):
        return pltpu.make_async_copy(tiles.at[i], tile_buf.at[i], tile_sem.at[i])

    for i in range(count):
        tile_copy(i).start()
    total[...] = jnp.zeros_like(total)

    def add(i, carry):
        tile_copy(i).wait()
        total[target[i] * upper + source[i]] += tile_buf[i].astype(F32)
        return carry

    lax.fori_loop(0, count, add, 0)
    here = row[0]
    for d in range(per_dev):
        for out, side in ((away, 1 - here), (mine, here)):
            first = (side * per_dev + d) * upper
            sums = jnp.zeros(out.shape[1:], F32)
            for k in range(upper):
                whole = total[first + k]
                high = whole.astype(BF16)
                low = (whole - high.astype(F32)).astype(BF16)
                sums += jnp.dot(known[k], high, preferred_element_type=F32)
                sums += jnp.dot(known[k], low, preferred_element_type=F32)
            out[d] = sums.astype(BF16)


def top_products(source, target, known, tiles, per_dev):
    count, depth, width = tiles.shape
    rows = known.shape[1]
    in_vmem = pl.BlockSpec(memory_space=pltpu.VMEM)
    in_smem = pl.BlockSpec(memory_space=pltpu.SMEM)
    row = lax.axis_index("prow").astype(jnp.int32)[None]
    return pl.pallas_call(
        functools.partial(top_kernel, per_dev),
        out_shape=[jax.ShapeDtypeStruct((per_dev, rows, width), BF16)] * 2,
        in_specs=[in_smem] * 3 + [in_vmem, pl.BlockSpec(memory_space=pl.ANY)],
        out_specs=[in_vmem] * 2,
        scratch_shapes=[
            pltpu.VMEM((count, depth, width), BF16),
            pltpu.VMEM((2 * per_dev * known.shape[0], depth, width), F32),
            pltpu.SemaphoreType.DMA((count,)),
        ],
        compiler_params=pltpu.CompilerParams(vmem_limit_bytes=60 * 1024 * 1024),
    )(row, source, target, known, tiles)


def solve_kernel(seed, mine, other, inverse, solved, rounded):
    for d in range(seed.shape[0]):
        sums = mine[d].astype(F32) + other[d].astype(F32)
        reduced = (seed[d] - sums).astype(BF16)
        x = lax.dot_general(reduced, inverse[d], (((1,), (1,)), ((), ())), preferred_element_type=F32)
        solved[d] = x
        rounded[d] = x.astype(BF16)


def solve(seed, mine, other, inverse):
    return pl.pallas_call(
        solve_kernel,
        out_shape=(jax.ShapeDtypeStruct(seed.shape, F32), jax.ShapeDtypeStruct(seed.shape, BF16)),
        in_specs=[pl.BlockSpec(memory_space=pltpu.VMEM)] * 4,
        out_specs=(pl.BlockSpec(memory_space=pltpu.VMEM),) * 2,
    )(seed, mine, other, inverse)


def swap(a, axis):
    return lax.ppermute(a, axis, [(0, 1), (1, 0)])


Z, Y, X = 4, 4, 2


def shift(a, **by):
    def at(z, y, x):
        return ((z % Z) * Y + y % Y) * X + x % X

    dz, dy, dx = by.get("z", 0), by.get("y", 0), by.get("x", 0)
    pairs = [(at(z, y, x), at(z + dz, y + dy, x + dx)) for z in range(Z) for y in range(Y) for x in range(X)]
    return lax.ppermute(a, "pcol", pairs)


def gather(rounded, beside=()):
    orders = (("y", "z"), ("z", "y"))
    across = shift(rounded, x=1)
    pairs = [jnp.concatenate([rounded[d : d + 1], across[d : d + 1]]) for d in range(2)]
    near = [[shift(pair, **{first: by}) for by in (1, -1, 2)] for pair, (first, _) in zip(pairs, orders)]
    planes = []
    for pair, others in zip(pairs, near):
        planes.append(jnp.concatenate([pair, *others]))
    planes = lax.optimization_barrier(planes)
    last = [(shift(plane, **{second: 1}), shift(plane, **{second: -1})) for plane, (_, second) in zip(planes, orders)]
    last, beside = lax.optimization_barrier((last, beside))
    half = planes[0].shape[0] // 2
    pieces = []
    for plane, (up, down), (_, second) in zip(planes, last, orders):
        pieces += [plane, up, down, shift(up[:half], **{second: 1}), shift(down[half:], **{second: -1})]
    return pieces, beside


def place_of(source, upper, n_top):
    per_dev = 2
    own = source - upper
    leaf, column, d = own // (n_top // 2), (own % (n_top // 2)) // per_dev, own % per_dev
    group = jnp.where(own >= n_top, 2, (leaf != lax.axis_index("leaf")).astype(jnp.int32))
    me = lax.axis_index("pcol")
    z = (column // (Y * X) - me // (Y * X)) % Z
    y = (column // X - me // X) % Y
    x = (column - me) % X
    first = jnp.where(d == 0, y, z)
    second = jnp.where(d == 0, z, y)
    nth = jnp.where(first == 0, 0, jnp.where(first == 3, 1, jnp.where(first == 1, 2, 3)))
    at = nth * X + x
    high = (second == 2) & (at >= 4)
    piece = jnp.where(second == 0, 0, jnp.where(second == 3, 1, jnp.where(second == 1, 2, jnp.where(high, 4, 3))))
    at = jnp.where(high, at - 4, at)
    piece = 1 + piece + 5 * d + 10 * group
    in_upper = source < upper
    return jnp.where(in_upper, 0, piece), jnp.where(in_upper, source, at)


N_STORES = 31


def plan(source, target, upper, n_top):
    piece, at = place_of(source, upper, n_top)
    key = ((target + 2 * lax.axis_index("prow") + 2) % 4) * N_STORES + piece
    count = source.shape[0]
    ids = jnp.arange(count, dtype=jnp.int32)
    before = (key[None, :] < key[:, None]) | ((key[None, :] == key[:, None]) & (ids[None, :] < ids[:, None]))
    rank = jnp.sum(before.astype(jnp.int32), axis=1)
    hit = (rank[None, :] == ids[:, None]).astype(jnp.int32)
    order, loc = jnp.sum(hit[None] * jnp.stack([ids, at])[:, None, :], axis=2)
    keys = jnp.arange(4 * N_STORES + 1, dtype=jnp.int32)
    starts = jnp.sum((key[None, :] < keys[:, None]).astype(jnp.int32), axis=1)
    return order, loc, starts


def local(
    known_above,
    seed_top,
    seed_mid,
    seed_low,
    inverse_top,
    middle_inverses,
    inverse_low,
    tiles_top,
    tiles_mid,
    tiles_low,
    top_source_rows,
    source_mid,
    lowest_source_rows,
    target_top,
    target_mid,
    target_low,
):
    known = known_above[0]
    seed_top, seed_mid, seed_low, inverse_top, middle_inverses, inverse_low = (
        a[0, 0, 0] for a in (seed_top, seed_mid, seed_low, inverse_top, middle_inverses, inverse_low)
    )
    tiles_top, tiles_mid, tiles_low = (a[0, 0, 0] for a in (tiles_top, tiles_mid, tiles_low))
    top_source, mid_source, low_source, top_target, mid_target, low_target = (
        a[0, 0, 0]
        for a in (top_source_rows, source_mid, lowest_source_rows, target_top, target_mid, target_low)
    )
    upper = known.shape[0]
    per_dev = seed_top.shape[0]
    n_top = lax.axis_size("leaf") * lax.axis_size("pcol") * per_dev

    away_keys, mine_keys = (0, N_STORES), (2 * N_STORES, 3 * N_STORES)

    def level(index, groups, stores, tiles, dtype, init=(None, None)):
        away = tile_products(index, away_keys, groups, stores, tiles, dtype, init[0])
        mine = tile_products(index, mine_keys, groups, stores, tiles, dtype, init[1])
        return away, mine

    away, mine = top_products(top_source, top_target, known, tiles_top, per_dev)
    solved_top, rounded_top = solve(seed_top, mine, swap(away, "prow"), inverse_top)
    rounded_top, mid_source, low_source = lax.optimization_barrier((rounded_top, mid_source, low_source))
    pieces, _ = gather(rounded_top)
    p0, p1 = pieces[:5], pieces[5:]
    whole = [p0[0], p1[0]]
    whole, direct, far = lax.optimization_barrier(
        (whole, (p0[1], p0[2], p1[1], p1[2]), (p0[3], p0[4], p1[3], p1[4]))
    )
    whole, direct, far = ([swap(piece, "leaf") for piece in some] for some in (whole, direct, far))
    swapped = [whole[0], *direct[:2], *far[:2], whole[1], *direct[2:], *far[2:]]
    stores = [known] + pieces + swapped
    early = [(p, p) for p in range(len(stores))]

    index = plan(mid_source, mid_target, upper, n_top)
    away, mine = level(index, early, stores, tiles_mid, BF16)
    solved_mid, rounded_mid = solve(seed_mid, mine, swap(away, "prow"), middle_inverses)

    index = plan(low_source, low_target, upper, n_top)
    init = level(index, early, stores, tiles_low, F32)
    arrived, init = gather(rounded_mid, init)
    late = [(len(stores) + p, p) for p in range(len(arrived))]
    away, mine = level(index, late, arrived, tiles_low, BF16, init)
    solved_low, _ = solve(seed_low, mine, swap(away, "prow"), inverse_low)
    return tuple(a[None, None, None] for a in (solved_top, solved_mid, solved_low))


def solution(mesh):
    whole = P("leaf", "prow", "pcol")
    in_specs = (P("prow"),) + (whole,) * 15
    return jax.shard_map(local, mesh=mesh, in_specs=in_specs, out_specs=(whole,) * 3, check_vma=False)
```

```python
import functools

import jax
import jax.numpy as jnp
from jax import lax
from jax.experimental import pallas as pl
from jax.experimental.pallas import tpu as pltpu
from jax.sharding import PartitionSpec as P

BF16 = jnp.bfloat16
F32 = jnp.float32


def products_kernel(columns, stores_of, with_init, *refs):
    order, loc, starts = refs[:3]
    n_stores = 1 + max(store for _, store in stores_of)
    stores = refs[3 : 3 + n_stores]
    refs = refs[3 + n_stores :]
    tiles, refs = refs[0], refs[1:]
    if with_init:
        init, refs = refs[0], refs[1:]
    out, row_buf, tile_buf, acc, sem = refs
    depth = tiles.shape[1]

    def at(i, n=1):
        return pl.ds(pl.multiple_of(i * depth, depth), n * depth)

    def row_copy(store, i):
        return pltpu.make_async_copy(stores[store].at[loc[i]], row_buf.at[:, at(i)], sem.at[i])

    def tile_copy(i):
        return pltpu.make_async_copy(tiles.at[order[i]], tile_buf.at[at(i)], sem.at[i])

    for base in columns:
        for group, store in stores_of:

            def issue(i, carry, store=store):
                tile_copy(i).start()
                row_copy(store, i).start()
                return carry

            lax.fori_loop(starts[base + group], starts[base + group + 1], issue, 0)

    if with_init:
        acc[...] = init[...]
    else:
        acc[...] = jnp.zeros_like(acc)

    for c, base in enumerate(columns):
        first = starts[base + stores_of[0][0]]
        last = starts[base + stores_of[-1][0] + 1]

        def multiply(i, n, c=c):
            for k in range(n):
                both = tile_buf.at[pl.ds(0, depth + row_buf.shape[0])]
                pltpu.make_async_copy(both, both, sem.at[i + k]).wait()
            acc[c] += jnp.dot(row_buf[:, at(i, n)], tile_buf[at(i, n)], preferred_element_type=F32)

        def several(j, carry, first=first, multiply=multiply):
            multiply(first + RUN * j, RUN)
            return carry

        runs = (last - first) // RUN
        lax.fori_loop(0, runs, several, 0)
        first = first + runs * RUN
        size = RUN // 2
        while size:

            def rest(j, carry, first=first, size=size, multiply=multiply):
                multiply(first, size)
                return carry

            some = (last - first) // size
            lax.fori_loop(0, some, rest, 0)
            first = first + some * size
            size //= 2
    out[...] = acc[...].astype(out.dtype)


RUN = 4


def tile_products(index, columns, stores_of, stores, tiles, out_dtype, init=None):
    order, loc, starts = index
    count, depth, width = tiles.shape
    rows = stores[0].shape[1]
    in_hbm = pl.BlockSpec(memory_space=pltpu.HBM)
    in_vmem = pl.BlockSpec(memory_space=pltpu.VMEM)
    in_smem = pl.BlockSpec(memory_space=pltpu.SMEM)
    operands = [order, loc, starts, *stores, tiles]
    specs = [in_smem] * 3 + [in_hbm] * (len(stores) + 1)
    if init is not None:
        operands.append(init)
        specs.append(in_vmem)
    return pl.pallas_call(
        functools.partial(products_kernel, tuple(columns), tuple(stores_of), init is not None),
        out_shape=jax.ShapeDtypeStruct((len(columns), rows, width), out_dtype),
        in_specs=specs,
        out_specs=in_vmem,
        scratch_shapes=[
            pltpu.VMEM((rows, count * depth), BF16),
            pltpu.VMEM((count * depth, width), BF16),
            pltpu.VMEM((len(columns), rows, width), F32),
            pltpu.SemaphoreType.DMA((count,)),
        ],
        compiler_params=pltpu.CompilerParams(vmem_limit_bytes=60 * 1024 * 1024),
        cost_estimate=pl.CostEstimate(
            flops=count * rows * depth * width, bytes_accessed=count * depth * width * 2, transcendentals=0
        ),
    )(*operands)


def top_kernel(side, source, target, known, tiles, out, tile_buf, total, tile_sem):
    count = tiles.shape[0]
    upper, per_dev = known.shape[0], out.shape[0]
    first = side[0] * per_dev

    def tile_copy(i):
        return pltpu.make_async_copy(tiles.at[i], tile_buf.at[i], tile_sem.at[i])

    def here(i):
        return (target[i] >= first) & (target[i] < first + per_dev)

    def fetch(i, carry):
        pl.when(here(i))(lambda: tile_copy(i).start())
        return carry

    def add(i, carry):
        @pl.when(here(i))
        def _():
            tile_copy(i).wait()
            total[(target[i] - first) * upper + source[i]] += tile_buf[i].astype(F32)

        return carry

    lax.fori_loop(0, count, fetch, 0)
    total[...] = jnp.zeros_like(total)
    lax.fori_loop(0, count, add, 0)
    for d in range(per_dev):
        sums = jnp.zeros(out.shape[1:], F32)
        for k in range(upper):
            whole = total[d * upper + k]
            high = whole.astype(BF16)
            low = (whole - high.astype(F32)).astype(BF16)
            sums += jnp.dot(known[k], high, preferred_element_type=F32)
            sums += jnp.dot(known[k], low, preferred_element_type=F32)
        out[d] = sums.astype(BF16)


def top_products(side, source, target, known, tiles, per_dev):
    count, depth, width = tiles.shape
    rows = known.shape[1]
    in_vmem = pl.BlockSpec(memory_space=pltpu.VMEM)
    in_smem = pl.BlockSpec(memory_space=pltpu.SMEM)
    return pl.pallas_call(
        top_kernel,
        out_shape=jax.ShapeDtypeStruct((per_dev, rows, width), BF16),
        in_specs=[in_smem] * 3 + [in_vmem, pl.BlockSpec(memory_space=pl.ANY)],
        out_specs=in_vmem,
        scratch_shapes=[
            pltpu.VMEM((count, depth, width), BF16),
            pltpu.VMEM((per_dev * known.shape[0], depth, width), F32),
            pltpu.SemaphoreType.DMA((count,)),
        ],
        compiler_params=pltpu.CompilerParams(vmem_limit_bytes=60 * 1024 * 1024),
    )(side.astype(jnp.int32)[None], source, target, known, tiles)


def solve_kernel(seed, mine, other, inverse, solved, rounded):
    for d in range(seed.shape[0]):
        sums = mine[d].astype(F32) + other[d].astype(F32)
        reduced = (seed[d] - sums).astype(BF16)
        x = lax.dot_general(reduced, inverse[d], (((1,), (1,)), ((), ())), preferred_element_type=F32)
        solved[d] = x
        rounded[d] = x.astype(BF16)


def solve(seed, mine, other, inverse):
    return pl.pallas_call(
        solve_kernel,
        out_shape=(jax.ShapeDtypeStruct(seed.shape, F32), jax.ShapeDtypeStruct(seed.shape, BF16)),
        in_specs=[pl.BlockSpec(memory_space=pltpu.VMEM)] * 4,
        out_specs=(pl.BlockSpec(memory_space=pltpu.VMEM),) * 2,
    )(seed, mine, other, inverse)


def swap(a, axis):
    return lax.ppermute(a, axis, [(0, 1), (1, 0)])


Z, Y, X = 4, 4, 2


def shift(a, **by):
    def at(z, y, x):
        return ((z % Z) * Y + y % Y) * X + x % X

    dz, dy, dx = by.get("z", 0), by.get("y", 0), by.get("x", 0)
    pairs = [(at(z, y, x), at(z + dz, y + dy, x + dx)) for z in range(Z) for y in range(Y) for x in range(X)]
    return lax.ppermute(a, "pcol", pairs)


def gather(rounded, beside=()):
    orders = (("y", "z"), ("z", "y"))
    across = shift(rounded, x=1)
    pairs = [jnp.concatenate([rounded[d : d + 1], across[d : d + 1]]) for d in range(2)]
    near = [[shift(pair, **{first: by}) for by in (1, -1, 2)] for pair, (first, _) in zip(pairs, orders)]
    planes = []
    for pair, others in zip(pairs, near):
        planes.append(jnp.concatenate([pair, *others]))
    planes = lax.optimization_barrier(planes)
    last = [(shift(plane, **{second: 1}), shift(plane, **{second: -1})) for plane, (_, second) in zip(planes, orders)]
    last, beside = lax.optimization_barrier((last, beside))
    half = planes[0].shape[0] // 2
    pieces = []
    for plane, (up, down), (_, second) in zip(planes, last, orders):
        pieces += [plane, up, down, shift(up[:half], **{second: 1}), shift(down[half:], **{second: -1})]
    return pieces, beside


def place_of(source, upper, n_top):
    per_dev = 2
    own = source - upper
    leaf, column, d = own // (n_top // 2), (own % (n_top // 2)) // per_dev, own % per_dev
    group = jnp.where(own >= n_top, 2, (leaf != lax.axis_index("leaf")).astype(jnp.int32))
    me = lax.axis_index("pcol")
    z = (column // (Y * X) - me // (Y * X)) % Z
    y = (column // X - me // X) % Y
    x = (column - me) % X
    first = jnp.where(d == 0, y, z)
    second = jnp.where(d == 0, z, y)
    nth = jnp.where(first == 0, 0, jnp.where(first == 3, 1, jnp.where(first == 1, 2, 3)))
    at = nth * X + x
    high = (second == 2) & (at >= 4)
    piece = jnp.where(second == 0, 0, jnp.where(second == 3, 1, jnp.where(second == 1, 2, jnp.where(high, 4, 3))))
    at = jnp.where(high, at - 4, at)
    piece = 1 + piece + 5 * d + 10 * group
    in_upper = source < upper
    return jnp.where(in_upper, 0, piece), jnp.where(in_upper, source, at)


N_STORES = 31


def plan(source, target, upper, n_top):
    piece, at = place_of(source, upper, n_top)
    key = ((target + 2 * lax.axis_index("prow") + 2) % 4) * N_STORES + piece
    count = source.shape[0]
    ids = jnp.arange(count, dtype=jnp.int32)
    before = (key[None, :] < key[:, None]) | ((key[None, :] == key[:, None]) & (ids[None, :] < ids[:, None]))
    rank = jnp.sum(before.astype(jnp.int32), axis=1)
    hit = (rank[None, :] == ids[:, None]).astype(jnp.int32)
    order, loc = jnp.sum(hit[None] * jnp.stack([ids, at])[:, None, :], axis=2)
    keys = jnp.arange(4 * N_STORES + 1, dtype=jnp.int32)
    starts = jnp.sum((key[None, :] < keys[:, None]).astype(jnp.int32), axis=1)
    return order, loc, starts


def local(
    known_above,
    seed_top,
    seed_mid,
    seed_low,
    inverse_top,
    middle_inverses,
    inverse_low,
    tiles_top,
    tiles_mid,
    tiles_low,
    top_source_rows,
    source_mid,
    lowest_source_rows,
    target_top,
    target_mid,
    target_low,
):
    known = known_above[0]
    seed_top, seed_mid, seed_low, inverse_top, middle_inverses, inverse_low = (
        a[0, 0, 0] for a in (seed_top, seed_mid, seed_low, inverse_top, middle_inverses, inverse_low)
    )
    tiles_top, tiles_mid, tiles_low = (a[0, 0, 0] for a in (tiles_top, tiles_mid, tiles_low))
    top_source, mid_source, low_source, top_target, mid_target, low_target = (
        a[0, 0, 0]
        for a in (top_source_rows, source_mid, lowest_source_rows, target_top, target_mid, target_low)
    )
    upper = known.shape[0]
    per_dev = seed_top.shape[0]
    n_top = lax.axis_size("leaf") * lax.axis_size("pcol") * per_dev

    away_keys, mine_keys = (0, N_STORES), (2 * N_STORES, 3 * N_STORES)

    def level(index, groups, stores, tiles, dtype, init=(None, None)):
        away = tile_products(index, away_keys, groups, stores, tiles, dtype, init[0])
        mine = tile_products(index, mine_keys, groups, stores, tiles, dtype, init[1])
        return away, mine

    row = lax.axis_index("prow")
    away, mine = (top_products(side, top_source, top_target, known, tiles_top, per_dev) for side in (1 - row, row))
    solved_top, rounded_top = solve(seed_top, mine, swap(away, "prow"), inverse_top)
    rounded_top, mid_source, low_source = lax.optimization_barrier((rounded_top, mid_source, low_source))
    pieces, _ = gather(rounded_top)
    p0, p1 = pieces[:5], pieces[5:]
    whole = [p0[0], p1[0]]
    whole, direct, far = lax.optimization_barrier(
        (whole, (p0[1], p0[2], p1[1], p1[2]), (p0[3], p0[4], p1[3], p1[4]))
    )
    whole, direct, far = ([swap(piece, "leaf") for piece in some] for some in (whole, direct, far))
    swapped = [whole[0], *direct[:2], *far[:2], whole[1], *direct[2:], *far[2:]]
    stores = [known] + pieces + swapped
    early = [(p, p) for p in range(len(stores))]

    index = plan(mid_source, mid_target, upper, n_top)
    away, mine = level(index, early, stores, tiles_mid, BF16)
    solved_mid, rounded_mid = solve(seed_mid, mine, swap(away, "prow"), middle_inverses)

    index = plan(low_source, low_target, upper, n_top)
    init = level(index, early, stores, tiles_low, F32)
    arrived, init = gather(rounded_mid, init)
    late = [(len(stores) + p, p) for p in range(len(arrived))]
    away, mine = level(index, late, arrived, tiles_low, BF16, init)
    solved_low, _ = solve(seed_low, mine, swap(away, "prow"), inverse_low)
    return tuple(a[None, None, None] for a in (solved_top, solved_mid, solved_low))


def solution(mesh):
    whole = P("leaf", "prow", "pcol")
    in_specs = (P("prow"),) + (whole,) * 15
    return jax.shard_map(local, mesh=mesh, in_specs=in_specs, out_specs=(whole,) * 3, check_vma=False)
```
